32 devices in a mesh: section: 4 (over y, core), dp: 4 (over z), mp: 2 (over x).
Axes of the slice: x: 2, y: 2, z: 4, core: 2. Of those that a mesh axis runs over, the one named last changes fastest.
Arguments:
- encoder_rows: bfloat16 [48, 256, 4096], P(('section', 'dp')), may hold values from -6 to 6
- w_key: bfloat16 [4096, 4096], P(('section', 'dp'), 'mp'), may hold values from -0.09375 to 0.09375
- w_value: bfloat16 [4096, 4096], P(('section', 'dp'), 'mp'), may hold values from -0.09375 to 0.09375
- query: bfloat16 [64, 128, 4096], P(('section', 'dp'), None, 'mp'), may hold values from -80 to 80
- grad_context: bfloat16 [64, 128, 4096], P(('section', 'dp'), None, 'mp'), may hold values from -6 to 6
- source: int32 [64], replicated, may hold values from 0 to 47, as said below
Outputs:
- context: bfloat16 [64, 128, 4096], P(('section', 'dp'), None, 'mp')
- grad_query: bfloat16 [64, 128, 4096], P(('section', 'dp'), None, 'mp')
- grad_kv_weights: float32 [2, 4096, 4096], P(None, ('section', 'dp'), 'mp')
The draws below stay inside these ranges and needn't reach their ends.
Inputs may be any that keep to these rules, and one draw needn't show every extreme that they name: `source`: the sequences of one section index (the 16 consecutive sequences held at that section index) read only examples held at the same section index; the 4 sequences of one device read examples held at 4 different dp indices.
All inputs are finite; a program needn't handle non-finite values.
Results may differ from the reference program's by a relative error of at most 0.025.
The reference program's roundings to bfloat16 on the way (of `keys`, `values`, `probs`, `score_grads`, `key_terms`, `value_terms`, `grad_keys` and `grad_values`) count: a program that leaves them out, or rounds other values in their place, can miss the bound.
Values may be sent and summed in bfloat16 or wider, within the bound.
No kernel may reach another device: no remote copies, remote signals or barrier semaphores. Data moves between devices by JAX's collectives and lax.ppermute only.
A program may use at most 192 MiB of HBM per device.

```python
import jax
import jax.numpy as jnp
from jax import lax

D = 4096
HEADS = 64
HEAD_DIM = 64
S = 256
TQ = 128
DSEQ = 4
EX_DEV = 3
EXAMPLES = 48
DEC_SEQS = 64
INNER = 4096
N_SECTION = 4
N_DP = 4


def draw_query(key, part):
    shape = (DEC_SEQS, TQ, HEADS * HEAD_DIM)
    return (0.15 * jax.random.truncated_normal(key, -6.0, 6.0, shape, jnp.float32)).astype(jnp.bfloat16)


def draw_source(key, part):
    groups = N_SECTION * N_DP
    split_keys = jax.random.split(jax.random.fold_in(key, 11), groups)
    owners = jax.vmap(lambda one: jax.random.permutation(one, N_DP))(split_keys)[:, :DSEQ]
    local = jax.random.randint(jax.random.fold_in(key, 12), (groups, DSEQ), 0, EX_DEV)
    section_of = (jnp.arange(groups, dtype=jnp.int32) // N_DP)[:, None]
    holder = section_of * N_DP + owners.astype(jnp.int32)
    return (holder * EX_DEV + local).reshape(-1).astype(jnp.int32)


def strengthened(result, key, source, target, parts, factor):
    owner, partner = [(jnp.arange(result.shape[axis_at]) // (result.shape[axis_at] // parts)).reshape([-1 if axis == axis_at else 1 for axis in range(result.ndim)]) for axis_at in (source, target)]
    chosen = jax.random.permutation(key, parts)[partner]
    strong = (owner == chosen) | (owner == (partner + parts // 2) % parts)
    return jnp.where(strong, factor * result, result)


def shard_levels(stream_key, extent, cuts, smallest, high):
    factor_of = 1.0
    for dim, blocks in cuts:
        heights = jax.random.uniform(jax.random.fold_in(jax.random.fold_in(stream_key, 6), dim), (blocks,), jnp.float32, smallest / len(cuts), high / len(cuts))
        factor_of = factor_of * jnp.repeat(jnp.exp(heights), extent[dim] // blocks).reshape((-1,) + (1,) * (len(extent) - 1 - dim))
    return factor_of


def bell_draw(rng, dims, scale, most, shards=(), kind=jnp.bfloat16):
    factor_of = shard_levels(rng, dims, shards, -0.22, 0.18) if shards else 1.0
    drawn = jax.random.normal(rng, dims, jnp.float32) * scale * factor_of
    return jnp.minimum(jnp.maximum(drawn, -most), most).astype(kind)


def heavy_noise(rng, extent, spread, reach, cuts, heavy, kind=jnp.bfloat16):
    values = spread * jax.random.normal(rng, extent, jnp.float32)
    if cuts:
        values = values * shard_levels(rng, extent, cuts, -0.22, 0.18)
    return jnp.clip(strengthened(values, jax.random.fold_in(rng, 3), *heavy), -reach, reach).astype(kind)


def setup_inputs(seed: int = 0) -> dict:
    key_of = jax.random.split(jax.random.key(seed), 7)
    return {
        "encoder_rows": heavy_noise(key_of[0], (EXAMPLES, S, D), 1.0, 6.0, ((0, 16),), (0, 2, 16, 2.0)),
        "w_key": bell_draw(key_of[1], (D, INNER), D ** -0.5, 0.09375, ((0, 16), (1, 2))),
        "w_value": bell_draw(key_of[2], (D, INNER), D ** -0.5, 0.09375, ((0, 16), (1, 2))),
        "query": draw_query(jax.random.fold_in(key_of[6], 71), 0),
        "grad_context": bell_draw(key_of[4], (DEC_SEQS, TQ, INNER), 1.0, 6.0, ((0, 16), (2, 2))),
        "source": draw_source(jax.random.fold_in(key_of[6], 71), 0),
    }


def attend(query_rows, key_rows, value_rows, grad_rows):
    qf = query_rows.astype(jnp.float32).reshape(TQ, HEADS, HEAD_DIM)
    kf = key_rows.astype(jnp.float32).reshape(S, HEADS, HEAD_DIM)
    vf = value_rows.astype(jnp.float32).reshape(S, HEADS, HEAD_DIM)
    gf = grad_rows.astype(jnp.float32).reshape(TQ, HEADS, HEAD_DIM)
    scores = jnp.einsum('thc,uhc->htu', qf, kf)
    top = jnp.max(scores, axis=-1, keepdims=True)
    expo = jnp.exp(scores - top)
    weights = expo / jnp.sum(expo, axis=-1, keepdims=True)
    probs = weights.astype(jnp.bfloat16)
    pf = probs.astype(jnp.float32)
    context = jnp.einsum('htu,uhc->thc', pf, vf).astype(jnp.bfloat16)
    dprobs = jnp.einsum('thc,uhc->htu', gf, vf)
    delta = jnp.sum(weights * dprobs, axis=-1, keepdims=True)
    score_grads = (weights * (dprobs - delta)).astype(jnp.bfloat16)
    sf = score_grads.astype(jnp.float32)
    grad_query = jnp.einsum('htu,uhc->thc', sf, kf).astype(jnp.bfloat16)
    key_terms = jnp.einsum('htu,thc->uhc', sf, qf).astype(jnp.bfloat16)
    value_terms = jnp.einsum('htu,thc->uhc', pf, gf).astype(jnp.bfloat16)
    inner = HEADS * HEAD_DIM
    return (context.reshape(TQ, inner), grad_query.reshape(TQ, inner),
            key_terms.reshape(S, inner), value_terms.reshape(S, inner))


def reference(encoder_rows, w_key, w_value, query, grad_context, source):
    inner = HEADS * HEAD_DIM
    flat = encoder_rows.reshape(EXAMPLES * S, D)
    keys = jnp.dot(flat, w_key, preferred_element_type=jnp.float32).astype(jnp.bfloat16).reshape(EXAMPLES, S, inner)
    values = jnp.dot(flat, w_value, preferred_element_type=jnp.float32).astype(jnp.bfloat16).reshape(EXAMPLES, S, inner)

    def one_sequence(index):
        example = source[index]
        key_rows = lax.dynamic_index_in_dim(keys, example, 0, keepdims=False)
        value_rows = lax.dynamic_index_in_dim(values, example, 0, keepdims=False)
        return attend(query[index], key_rows, value_rows, grad_context[index])

    context, grad_query, key_terms, value_terms = lax.map(one_sequence, jnp.arange(DEC_SEQS, dtype=jnp.int32))
    grad_keys = jax.ops.segment_sum(key_terms.astype(jnp.float32), source, num_segments=EXAMPLES).astype(jnp.bfloat16)
    grad_values = jax.ops.segment_sum(value_terms.astype(jnp.float32), source, num_segments=EXAMPLES).astype(jnp.bfloat16)
    groups = N_SECTION * N_DP
    flat_groups = flat.reshape(groups, EX_DEV * S, D)
    key_groups = grad_keys.reshape(groups, EX_DEV * S, inner)
    value_groups = grad_values.reshape(groups, EX_DEV * S, inner)

    def accumulate(totals, pieces):
        rows, key_part, value_part = pieces
        term_key = jnp.dot(rows.T, key_part, preferred_element_type=jnp.float32).astype(jnp.bfloat16)
        term_value = jnp.dot(rows.T, value_part, preferred_element_type=jnp.float32).astype(jnp.bfloat16)
        term_key, term_value = lax.optimization_barrier((term_key, term_value))
        return (totals[0] + term_key.astype(jnp.float32), totals[1] + term_value.astype(jnp.float32)), None

    start = (jnp.zeros((D, inner), jnp.float32), jnp.zeros((D, inner), jnp.float32))
    totals, unused = lax.scan(accumulate, start, (flat_groups, key_groups, value_groups))
    return context, grad_query, jnp.stack([totals[0], totals[1]], axis=0)
```

```python
import functools

import jax
import jax.numpy as jnp
from jax import lax
from jax.experimental import pallas as pl
from jax.experimental.pallas import tpu as pltpu
from jax.sharding import PartitionSpec as P

HEAD_DIM = 64
LANES = 128
CHUNKS = 2
MIB = 1024 * 1024
BF = jnp.bfloat16
F32 = jnp.float32


def dot(a, b, dims):
    return lax.dot_general(a, b, (dims, ((), ())), preferred_element_type=F32)


def params(mib):
    return pltpu.CompilerParams(vmem_limit_bytes=mib * MIB)


def pack_weights_kernel(chunks, cols, k_ref, v_ref, *outs):
    for c in range(chunks):
        outs[c][0, :, :cols] = k_ref[:, c * cols:(c + 1) * cols]
        outs[c][0, :, cols:] = v_ref[:, c * cols:(c + 1) * cols]


def pack_weights(me, w_key, w_value, n_section, chunks, cols):
    rows = w_key.shape[0]
    own = chunks * cols
    block = pl.BlockSpec((rows, own), lambda r, at: (0, at[0] ^ r))
    return pl.pallas_call(
        lambda at, *refs: pack_weights_kernel(chunks, cols, *refs),
        grid_spec=pltpu.PrefetchScalarGridSpec(
            num_scalar_prefetch=1,
            grid=(n_section,),
            in_specs=[block, block],
            out_specs=[pl.BlockSpec((1, rows, 2 * cols), lambda r, at: (r, 0, 0))] * chunks,
        ),
        out_shape=[jax.ShapeDtypeStruct((n_section, rows, 2 * cols), BF)] * chunks,
        compiler_params=params(32),
    )(me, w_key, w_value)


def pack_queries_kernel(n_section, chunks, cols, all_filled, n_dp, at, q_ref, g_ref, *outs):
    q, g = q_ref[0], g_ref[0]
    if not all_filled:
        keep = at[n_dp + pl.program_id(0)] > 0
        q = jnp.where(keep, q, jnp.zeros_like(q))
        g = jnp.where(keep, g, jnp.zeros_like(g))
    for s in range(n_section):
        for c in range(chunks):
            lo = (s * chunks + c) * cols
            outs[c][s, 0, 0] = q[:, lo:lo + cols]
            outs[c][s, 0, 1] = g[:, lo:lo + cols]


def pack_queries(slot, filled, query, grad, n_section, n_dp, chunks, cols):
    dec_dev, q_rows, inner = query.shape
    block = pl.BlockSpec((1, q_rows, inner), lambda p, at: (at[p], 0, 0))
    return pl.pallas_call(
        functools.partial(pack_queries_kernel, n_section, chunks, cols, n_dp == dec_dev, n_dp),
        grid_spec=pltpu.PrefetchScalarGridSpec(
            num_scalar_prefetch=1,
            grid=(n_dp,),
            in_specs=[block, block],
            out_specs=[
                pl.BlockSpec((n_section, 1, 2, q_rows, cols), lambda p, at: (0, p, 0, 0, 0))
            ] * chunks,
        ),
        out_shape=[jax.ShapeDtypeStruct((n_section, n_dp, 2, q_rows, cols), BF)] * chunks,
        compiler_params=params(32),
    )(jnp.concatenate([slot, filled]).astype(jnp.int32), query, grad)


def unpack_outputs_kernel(n_section, chunks, cols, at, *refs):
    ctx_ref, gq_ref = refs[chunks:]
    for s in range(n_section):
        for c in range(chunks):
            lo = (s * chunks + c) * cols
            ctx_ref[0, :, lo:lo + cols] = refs[c][s, 0, 0]
            gq_ref[0, :, lo:lo + cols] = refs[c][s, 0, 1]


def unpack_outputs(my_holder, parts, dec_dev):
    n_section, n_dp, _, q_rows, cols = parts[0].shape
    chunks = len(parts)
    inner = n_section * chunks * cols
    block = pl.BlockSpec((n_section, 1, 2, q_rows, cols), lambda j, at: (0, at[j], 0, 0, 0))
    out = pl.BlockSpec((1, q_rows, inner), lambda j, at: (j, 0, 0))
    return pl.pallas_call(
        functools.partial(unpack_outputs_kernel, n_section, chunks, cols),
        grid_spec=pltpu.PrefetchScalarGridSpec(
            num_scalar_prefetch=1,
            grid=(dec_dev,),
            in_specs=[block] * chunks,
            out_specs=[out, out],
        ),
        out_shape=[jax.ShapeDtypeStruct((dec_dev, q_rows, inner), BF)] * 2,
        compiler_params=params(32),
    )(my_holder, *parts)


def project_kernel(n_dp, n_section, at, x_ref, *refs):
    own, below, above = refs[0], refs[1:n_dp], refs[n_dp:2 * n_dp - 1]
    out_ref, w_ref = refs[2 * n_dp - 1:]
    dp, me = at[0], at[1]
    rows = own.shape[1]

    @pl.when(pl.program_id(0) == 0)
    def _():
        for r in range(n_section):
            w_ref[me ^ r, dp] = own[r]
        for k in range(1, n_dp):
            @pl.when(dp >= k)
            def _():
                for r in range(n_section):
                    w_ref[me ^ r, dp - k] = below[k - 1][r]

            @pl.when(dp + k < n_dp)
            def _():
                for r in range(n_section):
                    w_ref[me ^ r, dp + k] = above[k - 1][r]

    w = w_ref[...].reshape(n_section * n_dp * rows, own.shape[2])
    out_ref[...] = dot(x_ref[...], w, ((1,), (0,))).astype(BF)


def project(at, flat, own, below, above):
    n_section, rows, both = own.shape
    total, width = flat.shape
    n_dp = len(below) + 1
    tile = 512 if total % 512 == 0 else 256
    w_block = pl.BlockSpec((n_section, rows, both), lambda i, at: (0, 0, 0))
    return pl.pallas_call(
        functools.partial(project_kernel, n_dp, n_section),
        grid_spec=pltpu.PrefetchScalarGridSpec(
            num_scalar_prefetch=1,
            grid=(total // tile,),
            in_specs=[pl.BlockSpec((tile, width), lambda i, at: (i, 0))] + [w_block] * (2 * n_dp - 1),
            out_specs=pl.BlockSpec((tile, both), lambda i, at: (i, 0)),
            scratch_shapes=[pltpu.VMEM((n_section, n_dp, rows, both), BF)],
        ),
        out_shape=jax.ShapeDtypeStruct((total, both), BF),
        compiler_params=params(56),
        cost_estimate=pl.CostEstimate(
            flops=2 * total * width * both,
            bytes_accessed=2 * (total * width + 2 * width * both + total * both),
            transcendentals=0,
        ),
    )(at, flat, own, *below, *above)


def weight_grad_kernel(x_ref, g_ref, out_ref):
    both = out_ref.shape[1]
    g = g_ref[...].reshape(both, g_ref.shape[2])
    out_ref[0] = dot(g, x_ref[...], ((1,), (0,))).astype(BF)


def weight_grad(flat, dkv, n_section, n_dp):
    total, width = flat.shape
    both = 2 * dkv.shape[1]
    rows = width // (n_section * n_dp)
    return pl.pallas_call(
        weight_grad_kernel,
        grid=(n_dp, n_section),
        in_specs=[
            pl.BlockSpec((total, rows), lambda d, s: (0, s * n_dp + d)),
            pl.BlockSpec((2, dkv.shape[1], total), lambda d, s: (0, 0, 0)),
        ],
        out_specs=pl.BlockSpec((1, both, rows), lambda d, s: (d, 0, s)),
        out_shape=jax.ShapeDtypeStruct((n_dp, both, n_section * rows), BF),
        compiler_params=params(56),
        cost_estimate=pl.CostEstimate(
            flops=2 * total * width * both,
            bytes_accessed=2 * (total * width + width * both + total * both),
            transcendentals=0,
        ),
    )(flat, dkv)


def attend_kernel(seqs, ex_dev, seq_len, q_rows, local_ref, k_ref, v_ref, qg_ref,
                  out_ref, dkv_ref, dk_acc, dv_acc):
    section = pl.program_id(0)
    dk_acc[...] = jnp.zeros_like(dk_acc)
    dv_acc[...] = jnp.zeros_like(dv_acc)
    low = lax.broadcasted_iota(jnp.int32, (q_rows, LANES), 1) < HEAD_DIM

    def stack(rows):
        zero = jnp.zeros_like(rows)
        return jnp.concatenate([jnp.where(low, rows, zero), jnp.where(low, zero, rows)], axis=0)

    def merge(rows):
        return jnp.where(low, rows[:q_rows], rows[q_rows:])

    for i in range(seqs):
        at = local_ref[section * seqs + i]
        keys = k_ref[0, at]
        values = v_ref[0, at]
        q_two = stack(qg_ref[0, i, 0])
        g_two = stack(qg_ref[0, i, 1])
        scores = dot(q_two, keys, ((1,), (1,)))
        top = jnp.max(scores, axis=-1, keepdims=True)
        expo = jnp.exp(scores - top)
        weights = expo * (1.0 / jnp.sum(expo, axis=-1, keepdims=True))
        probs = weights.astype(BF)
        out_ref[0, i, 0] = merge(dot(probs, values, ((1,), (0,)))).astype(BF)
        dprobs = dot(g_two, values, ((1,), (1,)))
        delta = jnp.sum(weights * dprobs, axis=-1, keepdims=True)
        score_grads = (weights * (dprobs - delta)).astype(BF)
        out_ref[0, i, 1] = merge(dot(score_grads, keys, ((1,), (0,)))).astype(BF)
        dk_acc[at] += dot(q_two, score_grads, ((0,), (0,))).astype(BF).astype(F32)
        dv_acc[at] += dot(g_two, probs, ((0,), (0,))).astype(BF).astype(F32)

    for e in range(ex_dev):
        dkv_ref[0, :, e * seq_len:(e + 1) * seq_len] = dk_acc[e].astype(BF)
        dkv_ref[1, :, e * seq_len:(e + 1) * seq_len] = dv_acc[e].astype(BF)


def attend(local, kv, qg):
    n_section, ex_dev, seq_len, both = kv.shape
    seqs, q_rows, width = qg.shape[1], qg.shape[3], qg.shape[4]
    pairs = width // LANES
    rows = ex_dev * seq_len
    qg_block = pl.BlockSpec((1, seqs, 2, q_rows, LANES), lambda s, p, _: (s, 0, 0, 0, p))
    kv_block = (1, ex_dev, seq_len, LANES)
    return pl.pallas_call(
        functools.partial(attend_kernel, seqs, ex_dev, seq_len, q_rows),
        grid_spec=pltpu.PrefetchScalarGridSpec(
            num_scalar_prefetch=1,
            grid=(n_section, pairs),
            in_specs=[
                pl.BlockSpec(kv_block, lambda s, p, _: (s, 0, 0, p)),
                pl.BlockSpec(kv_block, lambda s, p, _: (s, 0, 0, pairs + p)),
                qg_block,
            ],
            out_specs=[
                qg_block,
                pl.BlockSpec((2, LANES, rows), lambda s, p, _: (0, p, s)),
            ],
            scratch_shapes=[
                pltpu.VMEM((ex_dev, LANES, seq_len), F32),
                pltpu.VMEM((ex_dev, LANES, seq_len), F32),
            ],
        ),
        out_shape=[
            jax.ShapeDtypeStruct(qg.shape, BF),
            jax.ShapeDtypeStruct((2, width, n_section * rows), BF),
        ],
        compiler_params=params(32),
        cost_estimate=pl.CostEstimate(
            flops=6 * 2 * n_section * seqs * pairs * 2 * q_rows * seq_len * LANES,
            bytes_accessed=2 * (2 * kv.size + 2 * qg.size),
            transcendentals=n_section * seqs * pairs * 2 * q_rows * seq_len,
        ),
    )(local, kv, kv, qg)


def finish_grads_kernel(chunks, cols, at, *refs):
    out_ref = refs[chunks]
    for c in range(chunks):
        for kv in range(2):
            block = refs[c][0, kv * cols:(kv + 1) * cols].astype(F32)
            out_ref[kv, :, c * cols:(c + 1) * cols] = block.T


def finish_grads(me, parts, cols):
    n_section, both, rows = parts[0].shape
    chunks = len(parts)
    own = chunks * cols
    return pl.pallas_call(
        functools.partial(finish_grads_kernel, chunks, cols),
        grid_spec=pltpu.PrefetchScalarGridSpec(
            num_scalar_prefetch=1,
            grid=(n_section,),
            in_specs=[pl.BlockSpec((1, both, rows), lambda r, at: (r, 0, 0))] * chunks,
            out_specs=pl.BlockSpec((2, rows, own), lambda r, at: (0, 0, at[0] ^ r)),
        ),
        out_shape=jax.ShapeDtypeStruct((2, rows, n_section * own), F32),
        compiler_params=params(32),
    )(me, *parts)


def section_swap(blocks):
    n_section = lax.axis_size("section")
    out = [blocks[0]]
    for r in range(1, n_section):
        out.append(lax.ppermute(blocks[r], "section", [(i, i ^ r) for i in range(n_section)]))
    return out


def gather_line(block):
    n = lax.axis_size("dp")
    below, above = [], []
    up = down = block
    for k in range(1, n):
        up = lax.ppermute(up, "dp", [(i, i + 1) for i in range(k - 1, n - 1)])
        down = lax.ppermute(down, "dp", [(i, i - 1) for i in range(1, n - k + 1)])
        below.append(up)
        above.append(down)
    return below, above


def scatter_line(part):
    n = lax.axis_size("dp")
    me = lax.axis_index("dp")

    def own(k):
        return lax.dynamic_index_in_dim(part, jnp.clip(me + k, 0, n - 1), 0, keepdims=False)

    up = down = None
    for k in range(n - 1, 0, -1):
        send_up = own(k) if up is None else own(k) + up
        send_down = own(-k) if down is None else own(-k) + down
        up = lax.ppermute(send_up, "dp", [(i, i + 1) for i in range(0, n - k)])
        down = lax.ppermute(send_down, "dp", [(i, i - 1) for i in range(k, n)])
    return (own(0).astype(F32) + up.astype(F32) + down.astype(F32)).astype(BF)


def spread_examples(rows):
    ex_dev, seq_len, width = rows.shape
    n_section, n_mp = lax.axis_size("section"), lax.axis_size("mp")
    mp_idx, me = lax.axis_index("mp"), lax.axis_index("section")
    part = seq_len // n_mp
    mine = lax.dynamic_slice_in_dim(rows, mp_idx * part, part, axis=1)
    if n_mp != 2 or n_section != 4:
        every = lax.all_gather(mine, ("section", "mp"), axis=0)
        every = every.reshape(n_section, n_mp, ex_dev, part, width).swapaxes(1, 2)
        return every.reshape(n_section, ex_dev, seq_len, width)
    core = [(i, i ^ 1) for i in range(4)]
    far = [(i, i ^ 2) for i in range(4)]
    swap = [(0, 1), (1, 0)]
    zero = jnp.int32(0)
    whole = jnp.zeros((n_section, ex_dev, seq_len, width), BF)

    def put(whole, piece, section, example, row):
        return lax.dynamic_update_slice(whole, piece[None], (section, example, row, zero))

    whole = put(whole, rows, me, zero, zero)
    whole = put(whole, lax.ppermute(rows, "section", core), me ^ 1, zero, zero)
    for e in range(ex_dev):
        at = jnp.int32(e)
        from_far = lax.ppermute(mine[e:e + 1], "section", far)
        from_side = lax.ppermute(from_far, "mp", swap)
        other_far = lax.ppermute(from_far, "section", core)
        other_side = lax.ppermute(from_side, "section", core)
        whole = put(whole, from_far, me ^ 2, at, mp_idx * part)
        whole = put(whole, other_far, me ^ 3, at, mp_idx * part)
        whole = put(whole, from_side, me ^ 2, at, (1 - mp_idx) * part)
        whole = put(whole, other_side, me ^ 3, at, (1 - mp_idx) * part)
    return whole


def per_device(encoder_rows, w_key, w_value, query, grad_context, source):
    ex_dev, seq_len, width = encoder_rows.shape
    dec_dev, q_rows, inner_dev = query.shape
    d_rows = w_key.shape[0]
    n_section, n_dp = lax.axis_size("section"), lax.axis_size("dp")
    section_idx, dp_idx = lax.axis_index("section"), lax.axis_index("dp")
    own = inner_dev // n_section
    chunks = min(CHUNKS, own // LANES)
    cols = own // chunks
    me = section_idx.reshape(1)
    at = jnp.stack([dp_idx, section_idx])

    plan = source.reshape(n_section, n_dp, dec_dev)
    holder = plan // ex_dev - jnp.arange(n_section, dtype=jnp.int32)[:, None, None] * n_dp
    reads_me = holder == dp_idx
    local = jnp.sum(jnp.where(reads_me, plan % ex_dev, 0), axis=-1).reshape(-1)
    my_holder = holder[section_idx, dp_idx]
    hit = my_holder[None, :] == jnp.arange(n_dp, dtype=jnp.int32)[:, None]
    slot = jnp.sum(jnp.where(hit, jnp.arange(dec_dev, dtype=jnp.int32)[None, :], 0), axis=1)
    filled = jnp.any(hit, axis=1)

    w_send = pack_weights(me, w_key, w_value, n_section, chunks, cols)
    w_own = [jnp.stack(section_swap(w)) for w in w_send]
    qg_send = pack_queries(slot, filled, query, grad_context, n_section, n_dp, chunks, cols)
    plane = spread_examples(encoder_rows)
    flat = plane.reshape(n_section * ex_dev * seq_len, width)

    outs, grads = [], []
    for c in range(chunks):
        below, above = gather_line(w_own[c])
        qg_all = lax.all_to_all(
            qg_send[c].reshape((n_section * n_dp,) + qg_send[c].shape[2:]),
            ("section", "dp"), split_axis=0, concat_axis=0, tiled=True,
        ).reshape(qg_send[c].shape)
        kv = project(at, flat, w_own[c], below, above)
        kv = kv.reshape(n_section, ex_dev, seq_len, 2 * cols)
        out, dkv = attend(local, kv, qg_all)
        part = weight_grad(flat, dkv, n_section, n_dp)
        total = scatter_line(part).reshape(2 * cols, n_section, d_rows)
        blocks = [
            lax.dynamic_index_in_dim(total, section_idx ^ r, 1, keepdims=False)
            for r in range(n_section)
        ]
        grads.append(jnp.stack(section_swap(blocks)))
        out = lax.all_to_all(
            out.reshape((n_section * n_dp,) + out.shape[2:]),
            ("section", "dp"), split_axis=0, concat_axis=0, tiled=True,
        )
        outs.append(out.reshape(qg_all.shape))

    context, grad_query = unpack_outputs(my_holder, outs, dec_dev)
    return context, grad_query, finish_grads(me, grads, cols)


def solution(mesh):
    return jax.shard_map(
        per_device,
        mesh=mesh,
        in_specs=(
            P(("section", "dp"), None, None),
            P(("section", "dp"), "mp"),
            P(("section", "dp"), "mp"),
            P(("section", "dp"), None, "mp"),
            P(("section", "dp"), None, "mp"),
            P(),
        ),
        out_specs=(
            P(("section", "dp"), None, "mp"),
            P(("section", "dp"), None, "mp"),
            P(None, ("section", "dp"), "mp"),
        ),
        check_vma=False,
    )
```

```python
import functools

import jax
import jax.numpy as jnp
from jax import lax
from jax.experimental import pallas as pl
from jax.experimental.pallas import tpu as pltpu
from jax.sharding import PartitionSpec as P

HEAD_DIM = 64
LANES = 128
CHUNKS = 2
MIB = 1024 * 1024
BF = jnp.bfloat16
F32 = jnp.float32


def dot(a, b, dims):
    return lax.dot_general(a, b, (dims, ((), ())), preferred_element_type=F32)


def params(mib):
    return pltpu.CompilerParams(vmem_limit_bytes=mib * MIB)


def pack_weights_kernel(chunks, cols, k_ref, v_ref, *outs):
    for c in range(chunks):
        outs[c][0, :, :cols] = k_ref[:, c * cols:(c + 1) * cols]
        outs[c][0, :, cols:] = v_ref[:, c * cols:(c + 1) * cols]


def pack_weights(me, w_key, w_value, n_section, chunks, cols):
    rows = w_key.shape[0]
    own = chunks * cols
    block = pl.BlockSpec((rows, own), lambda r, at: (0, at[0] ^ r))
    return pl.pallas_call(
        lambda at, *refs: pack_weights_kernel(chunks, cols, *refs),
        grid_spec=pltpu.PrefetchScalarGridSpec(
            num_scalar_prefetch=1,
            grid=(n_section,),
            in_specs=[block, block],
            out_specs=[pl.BlockSpec((1, rows, 2 * cols), lambda r, at: (r, 0, 0))] * chunks,
        ),
        out_shape=[jax.ShapeDtypeStruct((n_section, rows, 2 * cols), BF)] * chunks,
        compiler_params=params(32),
    )(me, w_key, w_value)


def pack_queries_kernel(n_section, all_filled, n_dp, at, q_ref, g_ref, *outs):
    q, g = q_ref[0], g_ref[0]
    if not all_filled:
        keep = at[n_dp + pl.program_id(0)] > 0
        q = jnp.where(keep, q, jnp.zeros_like(q))
        g = jnp.where(keep, g, jnp.zeros_like(g))
    chunks, cols = len(outs), outs[0].shape[-1]
    for s in range(n_section):
        for c in range(chunks):
            lo = (s * chunks + c) * cols
            outs[c][s, 0, 0] = q[:, lo:lo + cols]
            outs[c][s, 0, 1] = g[:, lo:lo + cols]


def pack_queries(slot, filled, query, grad, n_section, n_dp, chunks):
    dec_dev, q_rows, inner = query.shape
    cols = inner // (n_section * chunks)
    block = pl.BlockSpec((1, q_rows, inner), lambda p, at: (at[p], 0, 0))
    return pl.pallas_call(
        functools.partial(pack_queries_kernel, n_section, n_dp == dec_dev, n_dp),
        grid_spec=pltpu.PrefetchScalarGridSpec(
            num_scalar_prefetch=1,
            grid=(n_dp,),
            in_specs=[block, block],
            out_specs=[
                pl.BlockSpec((n_section, 1, 2, q_rows, cols), lambda p, at: (0, p, 0, 0, 0))
            ] * chunks,
        ),
        out_shape=[jax.ShapeDtypeStruct((n_section, n_dp, 2, q_rows, cols), BF)] * chunks,
        compiler_params=params(32),
    )(jnp.concatenate([slot, filled]).astype(jnp.int32), query, grad)


def unpack_outputs_kernel(n_section, chunks, cols, at, *refs):
    ctx_ref, gq_ref = refs[chunks * n_section:]
    me = at[0]
    for r in range(n_section):
        for c in range(chunks):
            block = refs[c * n_section + r]
            lo = pl.multiple_of(((me ^ r) * chunks + c) * cols, LANES)
            ctx_ref[0, :, pl.ds(lo, cols)] = block[0, 0]
            gq_ref[0, :, pl.ds(lo, cols)] = block[0, 1]


def unpack_outputs(me, distance, parts, dec_dev):
    chunks, n_section = len(parts), len(parts[0])
    _, _, q_rows, cols = parts[0][0].shape
    inner = n_section * chunks * cols
    block = pl.BlockSpec((1, 2, q_rows, cols), lambda j, at: (at[1 + j], 0, 0, 0))
    out = pl.BlockSpec((1, q_rows, inner), lambda j, at: (j, 0, 0))
    return pl.pallas_call(
        functools.partial(unpack_outputs_kernel, n_section, chunks, cols),
        grid_spec=pltpu.PrefetchScalarGridSpec(
            num_scalar_prefetch=1,
            grid=(dec_dev,),
            in_specs=[block] * (chunks * n_section),
            out_specs=[out, out],
        ),
        out_shape=[jax.ShapeDtypeStruct((dec_dev, q_rows, inner), BF)] * 2,
        compiler_params=params(32),
    )(jnp.concatenate([me, distance]), *[b for part in parts for b in part])


def project_kernel(n_dp, n_section, at, x_ref, all_ref, out_ref, w_ref):
    me = at[0]

    @pl.when(pl.program_id(0) == 0)
    def _():
        for d in range(n_dp):
            for r in range(n_section):
                w_ref[me ^ r, d] = all_ref[d, r]

    w = w_ref[...].reshape(x_ref.shape[1], out_ref.shape[1])
    out_ref[...] = dot(x_ref[...], w, ((1,), (0,))).astype(BF)


def project(me, flat, w_all):
    n_dp, n_section, rows, both = w_all.shape
    total, width = flat.shape
    tile = 512 if total % 512 == 0 else 256
    return pl.pallas_call(
        functools.partial(project_kernel, n_dp, n_section),
        grid_spec=pltpu.PrefetchScalarGridSpec(
            num_scalar_prefetch=1,
            grid=(total // tile,),
            in_specs=[
                pl.BlockSpec((tile, width), lambda i, at: (i, 0)),
                pl.BlockSpec(w_all.shape, lambda i, at: (0, 0, 0, 0)),
            ],
            out_specs=pl.BlockSpec((tile, both), lambda i, at: (i, 0)),
            scratch_shapes=[pltpu.VMEM((n_section, n_dp, rows, both), BF)],
        ),
        out_shape=jax.ShapeDtypeStruct((total, both), BF),
        compiler_params=params(56),
        cost_estimate=pl.CostEstimate(
            flops=2 * total * width * both,
            bytes_accessed=2 * (total * width + 2 * width * both + total * both),
            transcendentals=0,
        ),
    )(me, flat, w_all)


def weight_grad_kernel(n_section, rows, *refs):
    g_ref, out_ref = refs[n_section:]
    g = g_ref[...].reshape(out_ref.shape[0], g_ref.shape[2])
    for s in range(n_section):
        out_ref[:, s * rows:(s + 1) * rows] = dot(g, refs[s][...], ((1,), (0,))).astype(BF)


def weight_grad(flat, dkv, n_section, n_dp):
    total, width = flat.shape
    both = 2 * dkv.shape[1]
    rows = width // (n_section * n_dp)
    return pl.pallas_call(
        functools.partial(weight_grad_kernel, n_section, rows),
        grid=(n_dp,),
        in_specs=[
            pl.BlockSpec((total, rows), functools.partial(lambda s, d: (0, s * n_dp + d), s))
            for s in range(n_section)
        ] + [pl.BlockSpec((2, dkv.shape[1], total), lambda d: (0, 0, 0))],
        out_specs=pl.BlockSpec((both, n_section * rows), lambda d: (d, 0)),
        out_shape=jax.ShapeDtypeStruct((n_dp * both, n_section * rows), BF),
        compiler_params=params(56),
        cost_estimate=pl.CostEstimate(
            flops=2 * total * width * both,
            bytes_accessed=2 * (total * width + width * both + total * both),
            transcendentals=0,
        ),
    )(*([flat] * n_section), dkv)


def attend_kernel(seqs, ex_dev, seq_len, q_rows, local_ref, k_ref, v_ref, qg_ref,
                  out_ref, dkv_ref, dk_acc, dv_acc):
    section = pl.program_id(0)
    dk_acc[...] = jnp.zeros_like(dk_acc)
    dv_acc[...] = jnp.zeros_like(dv_acc)
    low = lax.broadcasted_iota(jnp.int32, (q_rows, LANES), 1) < HEAD_DIM

    def stack(rows):
        zero = jnp.zeros_like(rows)
        return jnp.concatenate([jnp.where(low, rows, zero), jnp.where(low, zero, rows)], axis=0)

    def merge(rows):
        return jnp.where(low, rows[:q_rows], rows[q_rows:])

    for i in range(seqs):
        at = local_ref[section * seqs + i]
        keys = k_ref[0, at]
        values = v_ref[0, at]
        q_two = stack(qg_ref[0, i, 0])
        g_two = stack(qg_ref[0, i, 1])
        scores = dot(q_two, keys, ((1,), (1,)))
        top = jnp.max(scores, axis=-1, keepdims=True)
        expo = jnp.exp(scores - top)
        weights = expo * (1.0 / jnp.sum(expo, axis=-1, keepdims=True))
        probs = weights.astype(BF)
        out_ref[0, i, 0] = merge(dot(probs, values, ((1,), (0,)))).astype(BF)
        dprobs = dot(g_two, values, ((1,), (1,)))
        delta = jnp.sum(weights * dprobs, axis=-1, keepdims=True)
        score_grads = (weights * (dprobs - delta)).astype(BF)
        out_ref[0, i, 1] = merge(dot(score_grads, keys, ((1,), (0,)))).astype(BF)
        dk_acc[at] += dot(q_two, score_grads, ((0,), (0,))).astype(BF).astype(F32)
        dv_acc[at] += dot(g_two, probs, ((0,), (0,))).astype(BF).astype(F32)

    for e in range(ex_dev):
        dkv_ref[0, :, e * seq_len:(e + 1) * seq_len] = dk_acc[e].astype(BF)
        dkv_ref[1, :, e * seq_len:(e + 1) * seq_len] = dv_acc[e].astype(BF)


def attend(local, kv, qg):
    n_section, ex_dev, seq_len, both = kv.shape
    seqs, q_rows, width = qg.shape[1], qg.shape[3], both // 2
    pairs = width // LANES
    rows = ex_dev * seq_len
    out_shape = qg.shape[:4] + (width,)
    qg_block = (1, seqs, 2, q_rows, LANES)
    kv_block = (1, ex_dev, seq_len, LANES)
    return pl.pallas_call(
        functools.partial(attend_kernel, seqs, ex_dev, seq_len, q_rows),
        grid_spec=pltpu.PrefetchScalarGridSpec(
            num_scalar_prefetch=1,
            grid=(n_section, pairs),
            in_specs=[
                pl.BlockSpec(kv_block, lambda s, p, _: (s, 0, 0, p)),
                pl.BlockSpec(kv_block, lambda s, p, _: (s, 0, 0, pairs + p)),
                pl.BlockSpec(qg_block, lambda s, p, _: (s, 0, 0, 0, p)),
            ],
            out_specs=[
                pl.BlockSpec(qg_block, lambda s, p, _: (s, 0, 0, 0, p)),
                pl.BlockSpec((2, LANES, rows), lambda s, p, _: (0, p, s)),
            ],
            scratch_shapes=[
                pltpu.VMEM((ex_dev, LANES, seq_len), F32),
                pltpu.VMEM((ex_dev, LANES, seq_len), F32),
            ],
        ),
        out_shape=[
            jax.ShapeDtypeStruct(out_shape, BF),
            jax.ShapeDtypeStruct((2, width, n_section * rows), BF),
        ],
        compiler_params=params(32),
        cost_estimate=pl.CostEstimate(
            flops=6 * 2 * n_section * seqs * pairs * 2 * q_rows * seq_len * LANES,
            bytes_accessed=2 * (2 * kv.size + 2 * qg.size),
            transcendentals=n_section * seqs * pairs * 2 * q_rows * seq_len,
        ),
    )(local, kv, kv, qg)


def finish_grads_kernel(n_section, chunks, cols, at, *refs):
    out_ref = refs[chunks * n_section]
    me = at[0]
    for c in range(chunks):
        for r in range(n_section):
            lo = pl.multiple_of(((me ^ r) * chunks + c) * cols, LANES)
            out_ref[0, :, pl.ds(lo, cols)] = refs[c * n_section + r][...].astype(F32).T


def finish_grads(me, parts, cols):
    chunks, n_section = len(parts), len(parts[0])
    rows = parts[0][0].shape[1]
    inner = n_section * chunks * cols
    return pl.pallas_call(
        functools.partial(finish_grads_kernel, n_section, chunks, cols),
        grid_spec=pltpu.PrefetchScalarGridSpec(
            num_scalar_prefetch=1,
            grid=(2,),
            in_specs=[pl.BlockSpec((cols, rows), lambda k, at: (k, 0))] * (chunks * n_section),
            out_specs=pl.BlockSpec((1, rows, inner), lambda k, at: (k, 0, 0)),
        ),
        out_shape=jax.ShapeDtypeStruct((2, rows, inner), F32),
        compiler_params=params(32),
    )(me, *[b for part in parts for b in part])


def section_swap(blocks):
    n_section = lax.axis_size("section")
    out = [blocks[0]]
    for r in range(1, n_section):
        out.append(lax.ppermute(blocks[r], "section", [(i, i ^ r) for i in range(n_section)]))
    return out


def to_owner_plane(out):
    n_dp = out.shape[1]
    dp_idx = lax.axis_index("dp")
    moved = []
    for k in range(n_dp):
        block = lax.dynamic_index_in_dim(out, (dp_idx + k) % n_dp, 1, keepdims=False)
        if k:
            block = lax.ppermute(block, "dp", [(i, (i + k) % n_dp) for i in range(n_dp)])
        moved.append(block)
    return moved


def to_owner_section(moved):
    me = lax.axis_index("section")
    return section_swap([
        jnp.stack([lax.dynamic_index_in_dim(b, me ^ r, 0, keepdims=False) for b in moved])
        for r in range(moved[0].shape[0])
    ])


def together(*values):
    return lax.optimization_barrier(values)


LAST_STEP = 3


def spread_examples(rows, first, last):
    ex_dev, seq_len, width = rows.shape
    n_section, n_mp = lax.axis_size("section"), lax.axis_size("mp")
    mp_idx, me = lax.axis_index("mp"), lax.axis_index("section")
    part = seq_len // n_mp
    mine = lax.dynamic_slice_in_dim(rows, mp_idx * part, part, axis=1)
    if n_mp != 2 or n_section != 4:
        every = lax.all_gather(mine, ("section", "mp"), axis=0)
        every = every.reshape(n_section, n_mp, ex_dev, part, width).swapaxes(1, 2)
        return every.reshape(n_section, ex_dev, seq_len, width), first, last
    core = [(i, i ^ 1) for i in range(4)]
    far = [(i, i ^ 2) for i in range(4)]
    swap = [(0, 1), (1, 0)]
    zero = jnp.int32(0)
    near, across = mp_idx * part, (1 - mp_idx) * part

    def put(whole, piece, r, example, row):
        return lax.dynamic_update_slice(whole, piece[None], (me ^ r, jnp.int32(example), row, zero))

    whole = put(jnp.zeros((n_section, ex_dev, seq_len, width), BF), rows, 0, 0, zero)
    from_far, from_side, other_far, other_side = [], [], [], []
    for step in range(ex_dev + 2):
        new = {}
        if step == 0:
            new["first"] = first
            new["peer"] = lax.ppermute(rows, "section", core)
        if step == LAST_STEP:
            new["last"] = last
        if step < ex_dev:
            new["far"] = lax.ppermute(mine[step:step + 1], "section", far)
        if 1 <= step <= ex_dev:
            e = step - 1
            new["side"] = lax.ppermute(from_far[e], "mp", swap)
            new["other_far"] = lax.ppermute(from_far[e], "section", core)
            whole = put(whole, from_far[e], 2, e, near)
        if step >= 2:
            e = step - 2
            new["other_side"] = lax.ppermute(from_side[e], "section", core)
            whole = put(whole, other_far[e], 3, e, near)
            whole = put(whole, from_side[e], 2, e, across)
        if step >= 3:
            whole = put(whole, other_side[step - 3], 3, step - 3, across)
        if step == ex_dev + 1:
            whole = put(whole, new["other_side"], 3, step - 2, across)
            break
        whole, mine, new = together(whole, mine, new)
        if step == 0:
            first = new["first"]
            whole = put(whole, new["peer"], 1, 0, zero)
        if step == LAST_STEP:
            last = new["last"]
        for name, into in (("far", from_far), ("side", from_side), ("other_far", other_far),
                           ("other_side", other_side)):
            if name in new:
                into.append(new[name])
    return whole, first, last


def per_device(encoder_rows, w_key, w_value, query, grad_context, source):
    ex_dev, seq_len, width = encoder_rows.shape
    dec_dev, q_rows, inner_dev = query.shape
    d_rows = w_key.shape[0]
    n_section, n_dp = lax.axis_size("section"), lax.axis_size("dp")
    section_idx, dp_idx = lax.axis_index("section"), lax.axis_index("dp")
    own = inner_dev // n_section
    chunks = min(CHUNKS, own // LANES)
    cols = own // chunks
    me = section_idx.reshape(1)

    plan = source.reshape(n_section, n_dp, dec_dev)
    holder = plan // ex_dev - jnp.arange(n_section, dtype=jnp.int32)[:, None, None] * n_dp
    reads_me = holder == dp_idx
    local = jnp.sum(jnp.where(reads_me, plan % ex_dev, 0), axis=-1).reshape(-1)
    my_holder = holder[section_idx, dp_idx]
    hit = my_holder[None, :] == jnp.arange(n_dp, dtype=jnp.int32)[:, None]
    slot = jnp.sum(jnp.where(hit, jnp.arange(dec_dev, dtype=jnp.int32)[None, :], 0), axis=1)
    filled = jnp.any(hit, axis=1)

    w_send = pack_weights(me, w_key, w_value, n_section, chunks, cols)
    qg_all = [
        lax.all_to_all(
            qg.reshape((n_section * n_dp,) + qg.shape[2:]),
            ("section", "dp"), split_axis=0, concat_axis=0, tiled=True,
        ).reshape(qg.shape)
        for qg in pack_queries(slot, filled, query, grad_context, n_section, n_dp, chunks)
    ]
    w_first = jnp.concatenate(section_swap([w_send[0][r] for r in range(n_section)]))
    plane, (w_first, qg_all[0]), qg_all[1:] = spread_examples(encoder_rows, (w_first, qg_all[0]), qg_all[1:])
    flat = plane.reshape(n_section * ex_dev * seq_len, width)

    outs, grads = [], []
    moved = None
    for c in range(chunks):
        w_own = w_first
        if c:
            w_mine = w_send[c]
            w_own = jnp.concatenate(section_swap([w_mine[r] for r in range(n_section)]))
        w_all = lax.all_gather(w_own, "dp", axis=0, tiled=True)
        w_all = w_all.reshape(n_dp, n_section, d_rows, 2 * cols)
        kv = project(me, flat, w_all)
        kv = kv.reshape(n_section, ex_dev, seq_len, 2 * cols)
        out, dkv = attend(local, kv, qg_all[c])
        if moved is not None:
            dkv, _ = together(dkv, moved)
        total = lax.psum_scatter(
            weight_grad(flat, dkv, n_section, n_dp), "dp", scatter_dimension=0, tiled=True
        )
        blocks = [
            lax.dynamic_slice_in_dim(total, (section_idx ^ r) * d_rows, d_rows, axis=1)
            for r in range(n_section)
        ]
        grads.append(section_swap(blocks))
        moved = to_owner_plane(out)
        outs.append(to_owner_section(moved))

    context, grad_query = unpack_outputs(me, (dp_idx - my_holder) % n_dp, outs, dec_dev)
    return context, grad_query, finish_grads(me, grads, cols)


def solution(mesh):
    return jax.shard_map(
        per_device,
        mesh=mesh,
        in_specs=(
            P(("section", "dp"), None, None),
            P(("section", "dp"), "mp"),
            P(("section", "dp"), "mp"),
            P(("section", "dp"), None, "mp"),
            P(("section", "dp"), None, "mp"),
            P(),
        ),
        out_specs=(
            P(("section", "dp"), None, "mp"),
            P(("section", "dp"), None, "mp"),
            P(None, ("section", "dp"), "mp"),
        ),
        check_vma=False,
    )
```

```python
import functools

import jax
import jax.numpy as jnp
from jax import lax
from jax.experimental import pallas as pl
from jax.experimental.pallas import tpu as pltpu
from jax.sharding import PartitionSpec as P

HEAD_DIM = 64
LANES = 128
CHUNKS = 2
MIB = 1024 * 1024
BF = jnp.bfloat16
F32 = jnp.float32


def dot(a, b, dims):
    return lax.dot_general(a, b, (dims, ((), ())), preferred_element_type=F32)


def params(mib):
    return pltpu.CompilerParams(vmem_limit_bytes=mib * MIB)


def pack_weights_kernel(chunks, cols, k_ref, v_ref, *outs):
    for c in range(chunks):
        outs[c][0, :, :cols] = k_ref[:, c * cols:(c + 1) * cols]
        outs[c][0, :, cols:] = v_ref[:, c * cols:(c + 1) * cols]


def pack_weights(me, w_key, w_value, n_section, chunks, cols):
    rows = w_key.shape[0]
    own = chunks * cols
    block = pl.BlockSpec((rows, own), lambda r, at: (0, at[0] ^ r))
    return pl.pallas_call(
        lambda at, *refs: pack_weights_kernel(chunks, cols, *refs),
        grid_spec=pltpu.PrefetchScalarGridSpec(
            num_scalar_prefetch=1,
            grid=(n_section,),
            in_specs=[block, block],
            out_specs=[pl.BlockSpec((1, rows, 2 * cols), lambda r, at: (r, 0, 0))] * chunks,
        ),
        out_shape=[jax.ShapeDtypeStruct((n_section, rows, 2 * cols), BF)] * chunks,
        compiler_params=params(32),
    )(me, w_key, w_value)


def pack_queries_kernel(n_section, all_filled, n_dp, at, q_ref, g_ref, *outs):
    q, g = q_ref[0], g_ref[0]
    if not all_filled:
        keep = at[n_dp + pl.program_id(0)] > 0
        q = jnp.where(keep, q, jnp.zeros_like(q))
        g = jnp.where(keep, g, jnp.zeros_like(g))
    chunks, cols = len(outs), outs[0].shape[-1]
    for s in range(n_section):
        for c in range(chunks):
            lo = (s * chunks + c) * cols
            outs[c][s, 0, 0] = q[:, lo:lo + cols]
            outs[c][s, 0, 1] = g[:, lo:lo + cols]


def pack_queries(slot, filled, query, grad, n_section, n_dp, chunks):
    dec_dev, q_rows, inner = query.shape
    cols = inner // (n_section * chunks)
    block = pl.BlockSpec((1, q_rows, inner), lambda p, at: (at[p], 0, 0))
    return pl.pallas_call(
        functools.partial(pack_queries_kernel, n_section, n_dp == dec_dev, n_dp),
        grid_spec=pltpu.PrefetchScalarGridSpec(
            num_scalar_prefetch=1,
            grid=(n_dp,),
            in_specs=[block, block],
            out_specs=[
                pl.BlockSpec((n_section, 1, 2, q_rows, cols), lambda p, at: (0, p, 0, 0, 0))
            ] * chunks,
        ),
        out_shape=[jax.ShapeDtypeStruct((n_section, n_dp, 2, q_rows, cols), BF)] * chunks,
        compiler_params=params(32),
    )(jnp.concatenate([slot, filled]).astype(jnp.int32), query, grad)


def unpack_outputs_kernel(n_section, chunks, cols, at, *refs):
    ctx_ref, gq_ref = refs[chunks * n_section:]
    me = at[0]
    for r in range(n_section):
        for c in range(chunks):
            block = refs[c * n_section + r]
            lo = pl.multiple_of(((me ^ r) * chunks + c) * cols, LANES)
            ctx_ref[0, :, pl.ds(lo, cols)] = block[0, 0]
            gq_ref[0, :, pl.ds(lo, cols)] = block[0, 1]


def unpack_outputs(me, distance, parts, dec_dev):
    chunks, n_section = len(parts), len(parts[0])
    _, _, q_rows, cols = parts[0][0].shape
    inner = n_section * chunks * cols
    block = pl.BlockSpec((1, 2, q_rows, cols), lambda j, at: (at[1 + j], 0, 0, 0))
    out = pl.BlockSpec((1, q_rows, inner), lambda j, at: (j, 0, 0))
    return pl.pallas_call(
        functools.partial(unpack_outputs_kernel, n_section, chunks, cols),
        grid_spec=pltpu.PrefetchScalarGridSpec(
            num_scalar_prefetch=1,
            grid=(dec_dev,),
            in_specs=[block] * (chunks * n_section),
            out_specs=[out, out],
        ),
        out_shape=[jax.ShapeDtypeStruct((dec_dev, q_rows, inner), BF)] * 2,
        compiler_params=params(32),
    )(jnp.concatenate([me, distance]), *[b for part in parts for b in part])


def project_kernel(n_dp, n_section, at, x_ref, all_ref, out_ref, w_ref):
    me = at[0]

    @pl.when(pl.program_id(0) == 0)
    def _():
        for d in range(n_dp):
            for r in range(n_section):
                w_ref[me ^ r, d] = all_ref[d, r]

    w = w_ref[...].reshape(x_ref.shape[1], out_ref.shape[1])
    out_ref[...] = dot(x_ref[...], w, ((1,), (0,))).astype(BF)


def project(me, flat, w_all):
    n_dp, n_section, rows, both = w_all.shape
    total, width = flat.shape
    tile = 512 if total % 512 == 0 else 256
    return pl.pallas_call(
        functools.partial(project_kernel, n_dp, n_section),
        grid_spec=pltpu.PrefetchScalarGridSpec(
            num_scalar_prefetch=1,
            grid=(total // tile,),
            in_specs=[
                pl.BlockSpec((tile, width), lambda i, at: (i, 0)),
                pl.BlockSpec(w_all.shape, lambda i, at: (0, 0, 0, 0)),
            ],
            out_specs=pl.BlockSpec((tile, both), lambda i, at: (i, 0)),
            scratch_shapes=[pltpu.VMEM((n_section, n_dp, rows, both), BF)],
        ),
        out_shape=jax.ShapeDtypeStruct((total, both), BF),
        compiler_params=params(56),
        cost_estimate=pl.CostEstimate(
            flops=2 * total * width * both,
            bytes_accessed=2 * (total * width + 2 * width * both + total * both),
            transcendentals=0,
        ),
    )(me, flat, w_all)


def weight_grad_kernel(n_section, at, *refs):
    g_ref, out_ref = refs[n_section:]
    g = g_ref[...].reshape(out_ref.shape[1], g_ref.shape[2])
    for r in range(n_section):
        out_ref[r] = dot(g, refs[r][...], ((1,), (0,))).astype(BF)


def weight_grad(me, flat, dkv, n_section, n_dp):
    total, width = flat.shape
    both = 2 * dkv.shape[1]
    rows = width // (n_section * n_dp)
    return pl.pallas_call(
        functools.partial(weight_grad_kernel, n_section),
        grid_spec=pltpu.PrefetchScalarGridSpec(
            num_scalar_prefetch=1,
            grid=(n_dp,),
            in_specs=[
                pl.BlockSpec((total, rows), functools.partial(lambda r, d, at: (0, (at[0] ^ r) * n_dp + d), r))
                for r in range(n_section)
            ] + [pl.BlockSpec((2, dkv.shape[1], total), lambda d, at: (0, 0, 0))],
            out_specs=pl.BlockSpec((n_section, both, rows), lambda d, at: (d, 0, 0)),
        ),
        out_shape=jax.ShapeDtypeStruct((n_dp * n_section, both, rows), BF),
        compiler_params=params(56),
        cost_estimate=pl.CostEstimate(
            flops=2 * total * width * both,
            bytes_accessed=2 * (total * width + width * both + total * both),
            transcendentals=0,
        ),
    )(me, *([flat] * n_section), dkv)


def attend_kernel(seqs, ex_dev, seq_len, q_rows, local_ref, k_ref, v_ref, qg_ref,
                  out_ref, dkv_ref, dk_acc, dv_acc):
    section = pl.program_id(0)
    dk_acc[...] = jnp.zeros_like(dk_acc)
    dv_acc[...] = jnp.zeros_like(dv_acc)
    low = lax.broadcasted_iota(jnp.int32, (q_rows, LANES), 1) < HEAD_DIM

    def stack(rows):
        zero = jnp.zeros_like(rows)
        return jnp.concatenate([jnp.where(low, rows, zero), jnp.where(low, zero, rows)], axis=0)

    def merge(rows):
        return jnp.where(low, rows[:q_rows], rows[q_rows:])

    for i in range(seqs):
        at = local_ref[section * seqs + i]
        keys = k_ref[0, at]
        values = v_ref[0, at]
        q_two = stack(qg_ref[0, i, 0])
        g_two = stack(qg_ref[0, i, 1])
        scores = dot(q_two, keys, ((1,), (1,)))
        top = jnp.max(scores, axis=-1, keepdims=True)
        expo = jnp.exp(scores - top)
        weights = expo * (1.0 / jnp.sum(expo, axis=-1, keepdims=True))
        probs = weights.astype(BF)
        out_ref[0, i, 0] = merge(dot(probs, values, ((1,), (0,)))).astype(BF)
        dprobs = dot(g_two, values, ((1,), (1,)))
        delta = jnp.sum(weights * dprobs, axis=-1, keepdims=True)
        score_grads = (weights * (dprobs - delta)).astype(BF)
        out_ref[0, i, 1] = merge(dot(score_grads, keys, ((1,), (0,)))).astype(BF)
        dk_acc[at] += dot(q_two, score_grads, ((0,), (0,))).astype(BF).astype(F32)
        dv_acc[at] += dot(g_two, probs, ((0,), (0,))).astype(BF).astype(F32)

    for e in range(ex_dev):
        dkv_ref[0, :, e * seq_len:(e + 1) * seq_len] = dk_acc[e].astype(BF)
        dkv_ref[1, :, e * seq_len:(e + 1) * seq_len] = dv_acc[e].astype(BF)


def attend(local, kv, qg):
    n_section, ex_dev, seq_len, both = kv.shape
    seqs, q_rows, width = qg.shape[1], qg.shape[3], both // 2
    pairs = width // LANES
    rows = ex_dev * seq_len
    out_shape = qg.shape[:4] + (width,)
    qg_block = (1, seqs, 2, q_rows, LANES)
    kv_block = (1, ex_dev, seq_len, LANES)
    return pl.pallas_call(
        functools.partial(attend_kernel, seqs, ex_dev, seq_len, q_rows),
        grid_spec=pltpu.PrefetchScalarGridSpec(
            num_scalar_prefetch=1,
            grid=(n_section, pairs),
            in_specs=[
                pl.BlockSpec(kv_block, lambda s, p, _: (s, 0, 0, p)),
                pl.BlockSpec(kv_block, lambda s, p, _: (s, 0, 0, pairs + p)),
                pl.BlockSpec(qg_block, lambda s, p, _: (s, 0, 0, 0, p)),
            ],
            out_specs=[
                pl.BlockSpec(qg_block, lambda s, p, _: (s, 0, 0, 0, p)),
                pl.BlockSpec((2, LANES, rows), lambda s, p, _: (0, p, s)),
            ],
            scratch_shapes=[
                pltpu.VMEM((ex_dev, LANES, seq_len), F32),
                pltpu.VMEM((ex_dev, LANES, seq_len), F32),
            ],
        ),
        out_shape=[
            jax.ShapeDtypeStruct(out_shape, BF),
            jax.ShapeDtypeStruct((2, width, n_section * rows), BF),
        ],
        compiler_params=params(32),
        cost_estimate=pl.CostEstimate(
            flops=6 * 2 * n_section * seqs * pairs * 2 * q_rows * seq_len * LANES,
            bytes_accessed=2 * (2 * kv.size + 2 * qg.size),
            transcendentals=n_section * seqs * pairs * 2 * q_rows * seq_len,
        ),
    )(local, kv, kv, qg)


def finish_grads_kernel(n_section, chunks, cols, at, *refs):
    out_ref = refs[chunks * n_section]
    me = at[0]
    for c in range(chunks):
        for r in range(n_section):
            lo = pl.multiple_of(((me ^ r) * chunks + c) * cols, LANES)
            out_ref[0, :, pl.ds(lo, cols)] = refs[c * n_section + r][...].astype(F32).T


def finish_grads(me, parts, cols, rows):
    chunks, n_section = len(parts), len(parts[0])
    inner = n_section * chunks * cols
    return pl.pallas_call(
        functools.partial(finish_grads_kernel, n_section, chunks, cols),
        grid_spec=pltpu.PrefetchScalarGridSpec(
            num_scalar_prefetch=1,
            grid=(2,),
            in_specs=[pl.BlockSpec((cols, rows), lambda k, at: (k, 0))] * (chunks * n_section),
            out_specs=pl.BlockSpec((1, rows, inner), lambda k, at: (k, 0, 0)),
        ),
        out_shape=jax.ShapeDtypeStruct((2, rows, inner), F32),
        compiler_params=params(32),
    )(me, *[b for part in parts for b in part])


def section_swap(blocks):
    n_section = lax.axis_size("section")
    out = [blocks[0]]
    for r in range(1, n_section):
        out.append(lax.ppermute(blocks[r], "section", [(i, i ^ r) for i in range(n_section)]))
    return out


def to_owner_plane(out):
    n_dp = out.shape[1]
    dp_idx = lax.axis_index("dp")
    moved = []
    for k in range(n_dp):
        block = lax.dynamic_index_in_dim(out, (dp_idx + k) % n_dp, 1, keepdims=False)
        if k:
            block = lax.ppermute(block, "dp", [(i, (i + k) % n_dp) for i in range(n_dp)])
        moved.append(block)
    return moved


def to_owner_section(moved):
    me = lax.axis_index("section")
    return section_swap([
        jnp.stack([lax.dynamic_index_in_dim(b, me ^ r, 0, keepdims=False) for b in moved])
        for r in range(moved[0].shape[0])
    ])


def together(*values):
    return lax.optimization_barrier(values)


def my_share(rows):
    part = rows.shape[1] // lax.axis_size("mp")
    return lax.dynamic_slice_in_dim(rows, lax.axis_index("mp") * part, part, axis=1)


def spread_examples(rows, mine, due):
    ex_dev, seq_len, width = rows.shape
    n_section, n_mp = lax.axis_size("section"), lax.axis_size("mp")
    mp_idx, me = lax.axis_index("mp"), lax.axis_index("section")
    part = seq_len // n_mp
    if n_mp != 2 or n_section != 4:
        every = lax.all_gather(mine, ("section", "mp"), axis=0)
        every = every.reshape(n_section, n_mp, ex_dev, part, width).swapaxes(1, 2)
        return every.reshape(n_section, ex_dev, seq_len, width), due
    core = [(i, i ^ 1) for i in range(4)]
    far = [(i, i ^ 2) for i in range(4)]
    swap = [(0, 1), (1, 0)]
    zero = jnp.int32(0)
    near, across = mp_idx * part, (1 - mp_idx) * part

    def put(whole, piece, r, example, row):
        return lax.dynamic_update_slice(whole, piece[None], (me ^ r, jnp.int32(example), row, zero))

    whole = put(jnp.zeros((n_section, ex_dev, seq_len, width), BF), rows, 0, 0, zero)
    from_far, from_side, other_far, other_side = [], [], [], []
    for step in range(ex_dev + 2):
        new = {}
        if step == 0:
            new["peer"] = lax.ppermute(rows, "section", core)
        if step in due:
            new["due"] = due[step]
        if step < ex_dev:
            new["far"] = lax.ppermute(mine[step:step + 1], "section", far)
        if 1 <= step <= ex_dev:
            e = step - 1
            new["side"] = lax.ppermute(from_far[e], "mp", swap)
            new["other_far"] = lax.ppermute(from_far[e], "section", core)
            whole = put(whole, from_far[e], 2, e, near)
        if step >= 2:
            e = step - 2
            new["other_side"] = lax.ppermute(from_side[e], "section", core)
            whole = put(whole, other_far[e], 3, e, near)
            whole = put(whole, from_side[e], 2, e, across)
        if step >= 3:
            whole = put(whole, other_side[step - 3], 3, step - 3, across)
        if step == ex_dev + 1:
            whole = put(whole, new["other_side"], 3, step - 2, across)
            break
        whole, mine, new = together(whole, mine, new)
        if step == 0:
            whole = put(whole, new["peer"], 1, 0, zero)
        if step in due:
            due[step] = new["due"]
        for name, into in (("far", from_far), ("side", from_side), ("other_far", other_far),
                           ("other_side", other_side)):
            if name in new:
                into.append(new[name])
    return whole, due


def per_device(encoder_rows, w_key, w_value, query, grad_context, source):
    ex_dev, seq_len, width = encoder_rows.shape
    dec_dev, q_rows, inner_dev = query.shape
    d_rows = w_key.shape[0]
    n_section, n_dp = lax.axis_size("section"), lax.axis_size("dp")
    section_idx, dp_idx = lax.axis_index("section"), lax.axis_index("dp")
    own = inner_dev // n_section
    chunks = min(CHUNKS, own // LANES)
    cols = own // chunks
    me = section_idx.reshape(1)

    plan = source.reshape(n_section, n_dp, dec_dev)
    holder = plan // ex_dev - jnp.arange(n_section, dtype=jnp.int32)[:, None, None] * n_dp
    reads_me = holder == dp_idx
    local = jnp.sum(jnp.where(reads_me, plan % ex_dev, 0), axis=-1).reshape(-1)
    my_holder = holder[section_idx, dp_idx]
    hit = my_holder[None, :] == jnp.arange(n_dp, dtype=jnp.int32)[:, None]
    slot = jnp.sum(jnp.where(hit, jnp.arange(dec_dev, dtype=jnp.int32)[None, :], 0), axis=1)
    filled = jnp.any(hit, axis=1)

    w_send = pack_weights(me, w_key, w_value, n_section, chunks, cols)
    w_first = jnp.concatenate(section_swap([w_send[0][r] for r in range(n_section)]))
    qg_send = pack_queries(slot, filled, query, grad_context, n_section, n_dp, chunks)
    mine = my_share(encoder_rows)
    w_first, mine, qg_send = together(w_first, mine, qg_send)
    qg_all = [
        lax.all_to_all(
            qg.reshape((n_section * n_dp,) + qg.shape[2:]),
            ("section", "dp"), split_axis=0, concat_axis=0, tiled=True,
        ).reshape(qg.shape)
        for qg in qg_send
    ]
    plane, due = spread_examples(encoder_rows, mine, {3: qg_all[0]})
    qg_all[0] = due[3]
    flat = plane.reshape(n_section * ex_dev * seq_len, width)

    outs, totals = [], []
    moved = None
    for c in range(chunks):
        w_own = w_first
        if c:
            w_mine = w_send[c]
            w_own = jnp.concatenate(section_swap([w_mine[r] for r in range(n_section)]))
        w_all = lax.all_gather(w_own, "dp", axis=0, tiled=True)
        w_all = w_all.reshape(n_dp, n_section, d_rows, 2 * cols)
        kv = project(me, flat, w_all)
        kv = kv.reshape(n_section, ex_dev, seq_len, 2 * cols)
        out, dkv = attend(local, kv, qg_all[c])
        if c == 0:
            dkv, qg_all = together(dkv, qg_all)
        if moved is not None:
            dkv, _ = together(dkv, moved)
        part = weight_grad(me, flat, dkv, n_section, n_dp)
        totals.append(lax.psum_scatter(
            part.reshape(n_dp * n_section * 2 * cols, d_rows), "dp", scatter_dimension=0, tiled=True
        ))
        moved = to_owner_plane(out)
        outs.append(to_owner_section(moved))

    context, grad_query = unpack_outputs(me, (dp_idx - my_holder) % n_dp, outs, dec_dev)
    grads = []
    for total in totals:
        if grads:
            total, grads[-1] = together(total, grads[-1])
        blocks = [total] + [total[r * 2 * cols:(r + 1) * 2 * cols] for r in range(1, n_section)]
        grads.append(section_swap(blocks))
    return context, grad_query, finish_grads(me, grads, cols, d_rows)


def solution(mesh):
    return jax.shard_map(
        per_device,
        mesh=mesh,
        in_specs=(
            P(("section", "dp"), None, None),
            P(("section", "dp"), "mp"),
            P(("section", "dp"), "mp"),
            P(("section", "dp"), None, "mp"),
            P(("section", "dp"), None, "mp"),
            P(),
        ),
        out_specs=(
            P(("section", "dp"), None, "mp"),
            P(("section", "dp"), None, "mp"),
            P(None, ("section", "dp"), "mp"),
        ),
        check_vma=False,
    )
```

```python
import functools

import jax
import jax.numpy as jnp
from jax import lax
from jax.experimental import pallas as pl
from jax.experimental.pallas import tpu as pltpu
from jax.sharding import PartitionSpec as P

HEAD_DIM = 64
LANES = 128
CHUNKS = 2
MIB = 1024 * 1024
BF = jnp.bfloat16
F32 = jnp.float32


def dot(a, b, dims):
    return lax.dot_general(a, b, (dims, ((), ())), preferred_element_type=F32)


def params(mib):
    return pltpu.CompilerParams(vmem_limit_bytes=mib * MIB)


def pack_weights_kernel(chunks, cols, k_ref, v_ref, *outs):
    for c in range(chunks):
        outs[c][0, :, :cols] = k_ref[:, c * cols:(c + 1) * cols]
        outs[c][0, :, cols:] = v_ref[:, c * cols:(c + 1) * cols]


def pack_weights(me, w_key, w_value, n_section, chunks, cols):
    rows = w_key.shape[0]
    own = chunks * cols
    block = pl.BlockSpec((rows, own), lambda r, at: (0, at[0] ^ r))
    return pl.pallas_call(
        lambda at, *refs: pack_weights_kernel(chunks, cols, *refs),
        grid_spec=pltpu.PrefetchScalarGridSpec(
            num_scalar_prefetch=1,
            grid=(n_section,),
            in_specs=[block, block],
            out_specs=[pl.BlockSpec((1, rows, 2 * cols), lambda r, at: (r, 0, 0))] * chunks,
        ),
        out_shape=[jax.ShapeDtypeStruct((n_section, rows, 2 * cols), BF)] * chunks,
        compiler_params=params(32),
    )(me, w_key, w_value)


def pack_queries_kernel(n_section, all_filled, n_dp, at, q_ref, g_ref, *outs):
    q, g = q_ref[0], g_ref[0]
    if not all_filled:
        keep = at[n_dp + pl.program_id(0)] > 0
        q = jnp.where(keep, q, jnp.zeros_like(q))
        g = jnp.where(keep, g, jnp.zeros_like(g))
    chunks, cols = len(outs), outs[0].shape[-1]
    for s in range(n_section):
        for c in range(chunks):
            lo = (s * chunks + c) * cols
            outs[c][s, 0, 0] = q[:, lo:lo + cols]
            outs[c][s, 0, 1] = g[:, lo:lo + cols]


def pack_queries(slot, filled, query, grad, n_section, n_dp, chunks):
    dec_dev, q_rows, inner = query.shape
    cols = inner // (n_section * chunks)
    block = pl.BlockSpec((1, q_rows, inner), lambda p, at: (at[p], 0, 0))
    return pl.pallas_call(
        functools.partial(pack_queries_kernel, n_section, n_dp == dec_dev, n_dp),
        grid_spec=pltpu.PrefetchScalarGridSpec(
            num_scalar_prefetch=1,
            grid=(n_dp,),
            in_specs=[block, block],
            out_specs=[
                pl.BlockSpec((n_section, 1, 2, q_rows, cols), lambda p, at: (0, p, 0, 0, 0))
            ] * chunks,
        ),
        out_shape=[jax.ShapeDtypeStruct((n_section, n_dp, 2, q_rows, cols), BF)] * chunks,
        compiler_params=params(32),
    )(jnp.concatenate([slot, filled]).astype(jnp.int32), query, grad)


def unpack_outputs_kernel(n_section, chunks, cols, at, *refs):
    ctx_ref, gq_ref = refs[chunks * n_section:]
    me = at[0]
    for r in range(n_section):
        for c in range(chunks):
            block = refs[c * n_section + r]
            lo = pl.multiple_of(((me ^ r) * chunks + c) * cols, LANES)
            ctx_ref[0, :, pl.ds(lo, cols)] = block[0, 0]
            gq_ref[0, :, pl.ds(lo, cols)] = block[0, 1]


def unpack_outputs(me, distance, parts, dec_dev):
    chunks, n_section = len(parts), len(parts[0])
    _, _, q_rows, cols = parts[0][0].shape
    inner = n_section * chunks * cols
    block = pl.BlockSpec((1, 2, q_rows, cols), lambda j, at: (at[1 + j], 0, 0, 0))
    out = pl.BlockSpec((1, q_rows, inner), lambda j, at: (j, 0, 0))
    return pl.pallas_call(
        functools.partial(unpack_outputs_kernel, n_section, chunks, cols),
        grid_spec=pltpu.PrefetchScalarGridSpec(
            num_scalar_prefetch=1,
            grid=(dec_dev,),
            in_specs=[block] * (chunks * n_section),
            out_specs=[out, out],
        ),
        out_shape=[jax.ShapeDtypeStruct((dec_dev, q_rows, inner), BF)] * 2,
        compiler_params=params(32),
    )(jnp.concatenate([me, distance]), *[b for part in parts for b in part])


def project_kernel(n_dp, n_section, at, x_ref, all_ref, out_ref, w_ref):
    me = at[0]

    @pl.when(pl.program_id(0) == 0)
    def _():
        for d in range(n_dp):
            for r in range(n_section):
                w_ref[me ^ r, d] = all_ref[d, r]

    w = w_ref[...].reshape(x_ref.shape[1], out_ref.shape[1])
    out_ref[...] = dot(x_ref[...], w, ((1,), (0,))).astype(BF)


def project(me, flat, w_all):
    n_dp, n_section, rows, both = w_all.shape
    total, width = flat.shape
    tile = 512 if total % 512 == 0 else 256
    return pl.pallas_call(
        functools.partial(project_kernel, n_dp, n_section),
        grid_spec=pltpu.PrefetchScalarGridSpec(
            num_scalar_prefetch=1,
            grid=(total // tile,),
            in_specs=[
                pl.BlockSpec((tile, width), lambda i, at: (i, 0)),
                pl.BlockSpec(w_all.shape, lambda i, at: (0, 0, 0, 0)),
            ],
            out_specs=pl.BlockSpec((tile, both), lambda i, at: (i, 0)),
            scratch_shapes=[pltpu.VMEM((n_section, n_dp, rows, both), BF)],
        ),
        out_shape=jax.ShapeDtypeStruct((total, both), BF),
        compiler_params=params(56),
        cost_estimate=pl.CostEstimate(
            flops=2 * total * width * both,
            bytes_accessed=2 * (total * width + 2 * width * both + total * both),
            transcendentals=0,
        ),
    )(me, flat, w_all)


def weight_grad_kernel(n_section, at, *refs):
    g_ref, out_ref = refs[n_section:]
    g = g_ref[...].reshape(out_ref.shape[1], g_ref.shape[2])
    for r in range(n_section):
        out_ref[r] = dot(g, refs[r][...], ((1,), (0,))).astype(BF)


def weight_grad(me, flat, dkv, n_section, n_dp):
    total, width = flat.shape
    both = 2 * dkv.shape[1]
    rows = width // (n_section * n_dp)
    return pl.pallas_call(
        functools.partial(weight_grad_kernel, n_section),
        grid_spec=pltpu.PrefetchScalarGridSpec(
            num_scalar_prefetch=1,
            grid=(n_dp,),
            in_specs=[
                pl.BlockSpec((total, rows), functools.partial(lambda r, d, at: (0, (at[0] ^ r) * n_dp + d), r))
                for r in range(n_section)
            ] + [pl.BlockSpec((2, dkv.shape[1], total), lambda d, at: (0, 0, 0))],
            out_specs=pl.BlockSpec((n_section, both, rows), lambda d, at: (d, 0, 0)),
        ),
        out_shape=jax.ShapeDtypeStruct((n_dp * n_section, both, rows), BF),
        compiler_params=params(56),
        cost_estimate=pl.CostEstimate(
            flops=2 * total * width * both,
            bytes_accessed=2 * (total * width + width * both + total * both),
            transcendentals=0,
        ),
    )(me, *([flat] * n_section), dkv)


def attend_kernel(seqs, ex_dev, seq_len, q_rows, local_ref, k_ref, v_ref, qg_ref,
                  out_ref, dkv_ref, dk_acc, dv_acc):
    section = pl.program_id(0)
    dk_acc[...] = jnp.zeros_like(dk_acc)
    dv_acc[...] = jnp.zeros_like(dv_acc)
    low = lax.broadcasted_iota(jnp.int32, (q_rows, LANES), 1) < HEAD_DIM

    def stack(rows):
        zero = jnp.zeros_like(rows)
        return jnp.concatenate([jnp.where(low, rows, zero), jnp.where(low, zero, rows)], axis=0)

    def merge(rows):
        return jnp.where(low, rows[:q_rows], rows[q_rows:])

    for i in range(seqs):
        at = local_ref[section * seqs + i]
        keys = k_ref[0, at]
        values = v_ref[0, at]
        q_two = stack(qg_ref[0, i, 0])
        g_two = stack(qg_ref[0, i, 1])
        scores = dot(q_two, keys, ((1,), (1,)))
        top = jnp.max(scores, axis=-1, keepdims=True)
        expo = jnp.exp(scores - top)
        weights = expo * (1.0 / jnp.sum(expo, axis=-1, keepdims=True))
        probs = weights.astype(BF)
        out_ref[0, i, 0] = merge(dot(probs, values, ((1,), (0,)))).astype(BF)
        dprobs = dot(g_two, values, ((1,), (1,)))
        delta = jnp.sum(weights * dprobs, axis=-1, keepdims=True)
        score_grads = (weights * (dprobs - delta)).astype(BF)
        out_ref[0, i, 1] = merge(dot(score_grads, keys, ((1,), (0,)))).astype(BF)
        dk_acc[at] += dot(q_two, score_grads, ((0,), (0,))).astype(BF).astype(F32)
        dv_acc[at] += dot(g_two, probs, ((0,), (0,))).astype(BF).astype(F32)

    for e in range(ex_dev):
        dkv_ref[0, :, e * seq_len:(e + 1) * seq_len] = dk_acc[e].astype(BF)
        dkv_ref[1, :, e * seq_len:(e + 1) * seq_len] = dv_acc[e].astype(BF)


def attend(local, kv, qg):
    n_section, ex_dev, seq_len, both = kv.shape
    seqs, q_rows, width = qg.shape[1], qg.shape[3], both // 2
    pairs = width // LANES
    rows = ex_dev * seq_len
    out_shape = qg.shape[:4] + (width,)
    qg_block = (1, seqs, 2, q_rows, LANES)
    kv_block = (1, ex_dev, seq_len, LANES)
    return pl.pallas_call(
        functools.partial(attend_kernel, seqs, ex_dev, seq_len, q_rows),
        grid_spec=pltpu.PrefetchScalarGridSpec(
            num_scalar_prefetch=1,
            grid=(n_section, pairs),
            in_specs=[
                pl.BlockSpec(kv_block, lambda s, p, _: (s, 0, 0, p)),
                pl.BlockSpec(kv_block, lambda s, p, _: (s, 0, 0, pairs + p)),
                pl.BlockSpec(qg_block, lambda s, p, _: (s, 0, 0, 0, p)),
            ],
            out_specs=[
                pl.BlockSpec(qg_block, lambda s, p, _: (s, 0, 0, 0, p)),
                pl.BlockSpec((2, LANES, rows), lambda s, p, _: (0, p, s)),
            ],
            scratch_shapes=[
                pltpu.VMEM((ex_dev, LANES, seq_len), F32),
                pltpu.VMEM((ex_dev, LANES, seq_len), F32),
            ],
        ),
        out_shape=[
            jax.ShapeDtypeStruct(out_shape, BF),
            jax.ShapeDtypeStruct((2, width, n_section * rows), BF),
        ],
        compiler_params=params(32),
        cost_estimate=pl.CostEstimate(
            flops=6 * 2 * n_section * seqs * pairs * 2 * q_rows * seq_len * LANES,
            bytes_accessed=2 * (2 * kv.size + 2 * qg.size),
            transcendentals=n_section * seqs * pairs * 2 * q_rows * seq_len,
        ),
    )(local, kv, kv, qg)


def finish_grads_kernel(n_section, chunks, cols, at, *refs):
    out_ref = refs[chunks * n_section]
    me = at[0]
    for c in range(chunks):
        for r in range(n_section):
            lo = pl.multiple_of(((me ^ r) * chunks + c) * cols, LANES)
            out_ref[0, :, pl.ds(lo, cols)] = refs[c * n_section + r][...].astype(F32).T


def finish_grads(me, parts, cols, rows):
    chunks, n_section = len(parts), len(parts[0])
    inner = n_section * chunks * cols
    return pl.pallas_call(
        functools.partial(finish_grads_kernel, n_section, chunks, cols),
        grid_spec=pltpu.PrefetchScalarGridSpec(
            num_scalar_prefetch=1,
            grid=(2,),
            in_specs=[pl.BlockSpec((cols, rows), lambda k, at: (k, 0))] * (chunks * n_section),
            out_specs=pl.BlockSpec((1, rows, inner), lambda k, at: (k, 0, 0)),
        ),
        out_shape=jax.ShapeDtypeStruct((2, rows, inner), F32),
        compiler_params=params(32),
    )(me, *[b for part in parts for b in part])


def section_swap(blocks):
    n_section = lax.axis_size("section")
    out = [blocks[0]]
    for r in range(1, n_section):
        out.append(lax.ppermute(blocks[r], "section", [(i, i ^ r) for i in range(n_section)]))
    return out


def to_owner(out, k):
    n_dp = out.shape[1]
    block = lax.dynamic_index_in_dim(out, (lax.axis_index("dp") + k) % n_dp, 1, keepdims=False)
    if k == 0:
        return block
    return lax.ppermute(block, "dp", [(i, (i + k) % n_dp) for i in range(n_dp)])


def to_owner_section(moved):
    me = lax.axis_index("section")
    return section_swap([
        jnp.stack([lax.dynamic_index_in_dim(b, me ^ r, 0, keepdims=False) for b in moved])
        for r in range(moved[0].shape[0])
    ])


def together(*values):
    return lax.optimization_barrier(values)


def my_share(rows):
    part = rows.shape[1] // lax.axis_size("mp")
    return lax.dynamic_slice_in_dim(rows, lax.axis_index("mp") * part, part, axis=1)


def spread_examples(rows, mine, due):
    ex_dev, seq_len, width = rows.shape
    n_section, n_mp = lax.axis_size("section"), lax.axis_size("mp")
    mp_idx, me = lax.axis_index("mp"), lax.axis_index("section")
    part = seq_len // n_mp
    if n_mp != 2 or n_section != 4:
        every = lax.all_gather(mine, ("section", "mp"), axis=0)
        every = every.reshape(n_section, n_mp, ex_dev, part, width).swapaxes(1, 2)
        return every.reshape(n_section, ex_dev, seq_len, width), due
    core = [(i, i ^ 1) for i in range(4)]
    far = [(i, i ^ 2) for i in range(4)]
    swap = [(0, 1), (1, 0)]
    zero = jnp.int32(0)
    near, across = mp_idx * part, (1 - mp_idx) * part

    def put(whole, piece, r, example, row):
        return lax.dynamic_update_slice(whole, piece[None], (me ^ r, jnp.int32(example), row, zero))

    whole = put(jnp.zeros((n_section, ex_dev, seq_len, width), BF), rows, 0, 0, zero)
    from_far, from_side, other_far, other_side = [], [], [], []
    for step in range(ex_dev + 2):
        new = {}
        if step == 0:
            new["peer"] = lax.ppermute(rows, "section", core)
        if step in due:
            new["due"] = due[step]
        if step < ex_dev:
            new["far"] = lax.ppermute(mine[step:step + 1], "section", far)
        if 1 <= step <= ex_dev:
            e = step - 1
            new["side"] = lax.ppermute(from_far[e], "mp", swap)
            new["other_far"] = lax.ppermute(from_far[e], "section", core)
            whole = put(whole, from_far[e], 2, e, near)
        if step >= 2:
            e = step - 2
            new["other_side"] = lax.ppermute(from_side[e], "section", core)
            whole = put(whole, other_far[e], 3, e, near)
            whole = put(whole, from_side[e], 2, e, across)
        if step >= 3:
            whole = put(whole, other_side[step - 3], 3, step - 3, across)
        if step == ex_dev + 1:
            whole = put(whole, new["other_side"], 3, step - 2, across)
            break
        whole, mine, new = together(whole, mine, new)
        if step == 0:
            whole = put(whole, new["peer"], 1, 0, zero)
        if step in due:
            due[step] = new["due"]
        for name, into in (("far", from_far), ("side", from_side), ("other_far", other_far),
                           ("other_side", other_side)):
            if name in new:
                into.append(new[name])
    return whole, due


def per_device(encoder_rows, w_key, w_value, query, grad_context, source):
    ex_dev, seq_len, width = encoder_rows.shape
    dec_dev, q_rows, inner_dev = query.shape
    d_rows = w_key.shape[0]
    n_section, n_dp = lax.axis_size("section"), lax.axis_size("dp")
    section_idx, dp_idx = lax.axis_index("section"), lax.axis_index("dp")
    own = inner_dev // n_section
    chunks = min(CHUNKS, own // LANES)
    cols = own // chunks
    me = section_idx.reshape(1)

    plan = source.reshape(n_section, n_dp, dec_dev)
    holder = plan // ex_dev - jnp.arange(n_section, dtype=jnp.int32)[:, None, None] * n_dp
    reads_me = holder == dp_idx
    local = jnp.sum(jnp.where(reads_me, plan % ex_dev, 0), axis=-1).reshape(-1)
    my_holder = holder[section_idx, dp_idx]
    hit = my_holder[None, :] == jnp.arange(n_dp, dtype=jnp.int32)[:, None]
    slot = jnp.sum(jnp.where(hit, jnp.arange(dec_dev, dtype=jnp.int32)[None, :], 0), axis=1)
    filled = jnp.any(hit, axis=1)

    w_send = pack_weights(me, w_key, w_value, n_section, chunks, cols)
    w_first = jnp.concatenate(section_swap([w_send[0][r] for r in range(n_section)]))
    qg_send = pack_queries(slot, filled, query, grad_context, n_section, n_dp, chunks)
    mine = my_share(encoder_rows)
    w_first, mine, qg_send = together(w_first, mine, qg_send)
    qg_all = [
        lax.all_to_all(
            qg.reshape((n_section * n_dp,) + qg.shape[2:]),
            ("section", "dp"), split_axis=0, concat_axis=0, tiled=True,
        ).reshape(qg.shape)
        for qg in qg_send
    ]
    plane, due = spread_examples(encoder_rows, mine, {3: qg_all[0]})
    qg_all[0] = due[3]
    flat = plane.reshape(n_section * ex_dev * seq_len, width)

    outs, grads = [], []
    moved = None
    for c in range(chunks):
        w_own = w_first
        if c:
            w_mine = w_send[c]
            w_own = jnp.concatenate(section_swap([w_mine[r] for r in range(n_section)]))
        w_all = lax.all_gather(w_own, "dp", axis=0, tiled=True)
        w_all = w_all.reshape(n_dp, n_section, d_rows, 2 * cols)
        kv = project(me, flat, w_all)
        kv = kv.reshape(n_section, ex_dev, seq_len, 2 * cols)
        out, dkv = attend(local, kv, qg_all[c])
        if c == 0:
            dkv, qg_all = together(dkv, qg_all)
        moving = [to_owner(out, k) for k in range(n_dp)]
        part = weight_grad(me, flat, dkv, n_section, n_dp)
        if moved is not None:
            part, moved, moving[1] = together(part, moved, moving[1])
        moved = moving
        total = lax.psum_scatter(
            part.reshape(n_dp * n_section * 2 * cols, d_rows), "dp", scatter_dimension=0, tiled=True
        )
        if grads:
            moving, grads[-1] = together(moving, grads[-1])
        outs.append(to_owner_section(moving))
        total, outs[-1] = together(total, outs[-1])
        blocks = [total] + [total[r * 2 * cols:(r + 1) * 2 * cols] for r in range(1, n_section)]
        grads.append(section_swap(blocks))

    context, grad_query = unpack_outputs(me, (dp_idx - my_holder) % n_dp, outs, dec_dev)
    return context, grad_query, finish_grads(me, grads, cols, d_rows)


def solution(mesh):
    return jax.shard_map(
        per_device,
        mesh=mesh,
        in_specs=(
            P(("section", "dp"), None, None),
            P(("section", "dp"), "mp"),
            P(("section", "dp"), "mp"),
            P(("section", "dp"), None, "mp"),
            P(("section", "dp"), None, "mp"),
            P(),
        ),
        out_specs=(
            P(("section", "dp"), None, "mp"),
            P(("section", "dp"), None, "mp"),
            P(None, ("section", "dp"), "mp"),
        ),
        check_vma=False,
    )
```
